512 devices in a mesh: replica: 32 (over z, y_hi, core), fsdp: 16 (over x, y_lo).
Axes of the slice: x: 4, y: 8 (y_hi: 2, y_lo: 4; y = y_hi * 4 + y_lo), z: 8, core: 2. Of those that a mesh axis runs over, the one named last changes fastest.
Arguments:
- inputs: bfloat16 [32, 4096, 4096], P('replica', 'fsdp'), may hold values from -6 to 6
- targets: bfloat16 [32, 4096, 1024], P('replica', 'fsdp'), may hold values from -6 to 6
- local_weight: bfloat16 [32, 4096, 1024], P('replica', 'fsdp'), may hold values from -0.09375 to 0.09375
- outer_params: float32 [4, 4096, 1024], P(None, ('fsdp', 'replica')), may hold values from -0.09375 to 0.09375
- outer_moment: float32 [4, 4096, 1024], P(None, ('fsdp', 'replica')), may hold values from -0.06 to 0.06
- fragment: int32 [1], replicated, may hold values from 0 to 16383
Outputs:
- merged_weight: float32 [32, 4096, 1024], P('replica', 'fsdp')
- new_params: float32 [4, 4096, 1024], P(None, ('fsdp', 'replica'))
- new_moment: float32 [4, 4096, 1024], P(None, ('fsdp', 'replica'))
The draws below stay inside these ranges and needn't reach their ends.
All inputs are finite; a program needn't handle non-finite values.
Results may differ from the reference program's by a relative error of at most 0.0027.
Values may be sent and summed in bfloat16 or wider, within the bound.
No kernel may reach another device: no remote copies, remote signals or barrier semaphores. Data moves between devices by JAX's collectives and lax.ppermute only.
A program may use at most 64 MiB of HBM per device.

```python
import jax
import jax.numpy as jnp
from jax import lax

D = 4096
KV = 1024
NFRAG = 4
TOKENS = 4096
REPLICAS = 32


def block_scale(key, dims, split, low, top_value):
    factor_of, own = 1.0, jax.random.fold_in(key, 6)
    for dim, shards_of in split:
        steps = jnp.exp(jax.random.uniform(jax.random.fold_in(own, dim), (shards_of,), jnp.float32, low / len(split), top_value / len(split)))
        factor_of = factor_of * jnp.repeat(steps, dims[dim] // shards_of).reshape([-1 if axis == dim else 1 for axis in range(len(dims))])
    return factor_of


def normal_values(rng, shape, scale, bound, pieces=(), kind=jnp.bfloat16):
    loudness = block_scale(rng, shape, pieces, -0.22, 0.18) if pieces else 1.0
    drawn = jax.random.normal(rng, shape, jnp.float32) * scale * loudness
    return jnp.minimum(jnp.maximum(drawn, -bound), bound).astype(kind)


def setup_inputs(seed: int = 0) -> dict:
    splits = jax.random.split(jax.random.key(seed), 7)
    return {
        "inputs": normal_values(splits[0], (REPLICAS, TOKENS, D), 1.0, 6.0, ((0, 32), (1, 16))),
        "targets": normal_values(splits[1], (REPLICAS, TOKENS, KV), 1.0, 6.0, ((0, 32), (1, 16))),
        "local_weight": normal_values(splits[2], (REPLICAS, D, KV), D ** -0.5, 0.09375, ((0, 32), (1, 16))),
        "outer_params": normal_values(splits[3], (NFRAG, D, KV), D ** -0.5, 0.09375, ((1, 512),), jnp.float32),
        "outer_moment": normal_values(splits[4], (NFRAG, D, KV), 0.01, 0.06, ((1, 512),), jnp.float32),
        "fragment": jax.random.randint(splits[5], (1,), 0, 4096 * NFRAG).astype(jnp.int32),
    }


inner_rate = 1.0
outer_rate = 0.7
moment_keep = 0.9
merge_share = 0.5


def reference(inputs, targets, local_weight, outer_params, outer_moment, fragment):
    which = jnp.remainder(fragment[0], jnp.int32(outer_params.shape[0])).astype(jnp.int32)
    old_global = lax.dynamic_index_in_dim(outer_params, which, 0, keepdims=False)
    old_moment = lax.dynamic_index_in_dim(outer_moment, which, 0, keepdims=False)
    outer_grad = old_global - jnp.mean(local_weight.astype(jnp.float32), axis=0)
    moment = moment_keep * old_moment + outer_grad
    global_next = old_global - outer_rate * (outer_grad + moment_keep * moment)

    def inner_step(items):
        tokens, wanted, weight = items
        projected = jnp.dot(tokens, weight, preferred_element_type=jnp.float32)
        residual = (projected - wanted.astype(jnp.float32)).astype(jnp.bfloat16)
        gradient = jnp.dot(tokens.T, residual, preferred_element_type=jnp.float32) / tokens.shape[0]
        stepped = weight.astype(jnp.float32) - inner_rate * gradient
        return merge_share * stepped + (1.0 - merge_share) * global_next

    merged_weight = lax.map(inner_step, (inputs, targets, local_weight))
    new_params = lax.dynamic_update_index_in_dim(outer_params, global_next, which, 0)
    new_moment = lax.dynamic_update_index_in_dim(outer_moment, moment, which, 0)
    return merged_weight, new_params, new_moment
```

```python
import functools

import jax
import jax.numpy as jnp
from jax import lax
from jax.sharding import Mesh, PartitionSpec as P

inner_rate = 1.0
outer_rate = 0.7
moment_keep = 0.9
merge_share = 0.5

PARTS = (("z", 8), ("yh", 2), ("core", 2), ("x", 4), ("yl", 4))
REPLICA = ("z", "yh", "core")
FSDP = ("x", "yl")
CHUNKS = 2
WIRE = jnp.bfloat16


def exchange(blocks, axis):
    return lax.all_to_all(blocks, axis, 0, 0, tiled=True)


def gather(block, axis):
    n = lax.axis_size(axis)
    return exchange(jnp.broadcast_to(block[None], (n,) + block.shape), axis)


def outer_step(own_rows, g_piece, m_piece):
    nz, nh, nc = (lax.axis_size(a) for a in REPLICA)
    rows, width = own_rows.shape
    piece = rows // (nz * nh * nc)
    by_owner = own_rows.reshape(nz, nh, nc, piece, width).transpose(0, 2, 1, 3, 4)
    got = exchange(by_owner.reshape(nz * nc, nh, piece, width), ("z", "core"))
    part = jnp.sum(got.astype(jnp.float32), axis=0)
    half = lax.axis_index("yh")
    mine = lax.dynamic_index_in_dim(part, half, 0, keepdims=False)
    other = lax.dynamic_index_in_dim(part, 1 - half, 0, keepdims=False)
    summed = mine + lax.ppermute(other, "yh", [(0, 1), (1, 0)])
    outer_grad = g_piece - summed / (nz * nh * nc)
    moment = moment_keep * m_piece + outer_grad
    return g_piece - outer_rate * (outer_grad + moment_keep * moment), moment


def spread(global_keep, rows):
    nz, nh, nc = (lax.axis_size(a) for a in REPLICA)
    piece, width = global_keep.shape
    sent = global_keep.astype(WIRE)
    other = lax.ppermute(sent, "yh", [(0, 1), (1, 0)])
    first = lax.axis_index("yh") == 0
    pair = jnp.stack([jnp.where(first, sent, other), jnp.where(first, other, sent)])
    got = gather(pair, ("z", "core")).reshape(nz, nc, nh, piece, width)
    return got.transpose(0, 2, 1, 3, 4).reshape(rows, width).astype(jnp.float32)


def on_device(inputs, targets, local_weight, outer_params, outer_moment, fragment):
    which = jnp.remainder(fragment[0], jnp.int32(outer_params.shape[0]))
    own_rows, tokens, wanted = local_weight[0], inputs[0], targets[0]
    rows, width = own_rows.shape
    count = tokens.shape[0]
    nx, ny = lax.axis_size("x"), lax.axis_size("yl")
    part = width // CHUNKS

    block = exchange(
        tokens.reshape(count, nx, -1).transpose(1, 0, 2), "x"
    ).reshape(nx * count, -1)
    weights = [
        gather(own_rows[:, c * part : (c + 1) * part], "yl").reshape(ny * rows, part)
        for c in range(CHUNKS)
    ]

    g_piece = lax.dynamic_index_in_dim(outer_params, which, 0, keepdims=False)
    m_piece = lax.dynamic_index_in_dim(outer_moment, which, 0, keepdims=False)
    global_keep, moment_kept = outer_step(own_rows, g_piece, m_piece)
    global_next = spread(global_keep, rows)

    merged = []
    for c in range(CHUNKS):
        cols = slice(c * part, (c + 1) * part)
        shares = jnp.dot(block, weights[c], preferred_element_type=jnp.float32)
        got = exchange(shares.astype(WIRE).reshape(nx, count, part), "x")
        projected = jnp.sum(got.astype(jnp.float32), axis=0)
        residual = (projected - wanted[:, cols].astype(jnp.float32)).astype(jnp.bfloat16)
        all_residual = gather(residual, "x").reshape(nx * count, part)
        shares = lax.dot_general(
            block, all_residual, (((0,), (0,)), ((), ())), preferred_element_type=jnp.float32
        )
        got = exchange(shares.astype(WIRE).reshape(ny, rows, part), "yl")
        gradient = jnp.sum(got.astype(jnp.float32), axis=0) / (count * nx * ny)
        stepped = own_rows[:, cols].astype(jnp.float32) - inner_rate * gradient
        merged.append(merge_share * stepped + (1.0 - merge_share) * global_next[:, cols])
    merged = jnp.concatenate(merged, axis=1)
    new_params = lax.dynamic_update_index_in_dim(outer_params, global_keep, which, 0)
    new_moment = lax.dynamic_update_index_in_dim(outer_moment, moment_kept, which, 0)
    return (merged[None], new_params, new_moment)


def solution(mesh):
    names = tuple(n for n, _ in PARTS)
    fine = Mesh(mesh.devices.reshape([k for _, k in PARTS]), names)
    local = P(REPLICA, FSDP, None)
    outer = P(None, FSDP + REPLICA, None)
    return jax.shard_map(
        on_device,
        mesh=fine,
        in_specs=(local, local, local, outer, outer, P()),
        out_specs=(local, outer, outer),
        check_vma=False,
    )
```

```python
import functools

import jax
import jax.numpy as jnp
from jax import lax
from jax.experimental import pallas as pl
from jax.experimental.layout import Layout, with_layout_constraint
from jax.experimental.pallas import tpu as pltpu
from jax.sharding import Mesh, PartitionSpec as P

inner_rate = 1.0
outer_rate = 0.7
moment_keep = 0.9
merge_share = 0.5

PARTS = (("z", 8), ("yh", 2), ("core", 2), ("x", 4), ("yl", 4))
REPLICA = ("z", "yh", "core")
FSDP = ("x", "yl")
CUTS = (0, 384, 1024)
WIRE = jnp.float16
SHARE_UP = 32.0
GRAD_DOWN = 2.0**-8
EARLY = 30_000_000_000
VMEM_LIMIT = 12 << 20
VMEM = pl.BlockSpec(memory_space=pltpu.VMEM)
ANY = pl.BlockSpec(memory_space=pl.ANY)
SMEM = pl.BlockSpec(memory_space=pltpu.SMEM)


def exchange(blocks, axis):
    return lax.all_to_all(blocks, axis, 0, 0, tiled=True)


def rowwise(x):
    return with_layout_constraint(x, Layout(tuple(range(x.ndim))))


def shift(block, axis, s):
    n = lax.axis_size(axis)
    return lax.ppermute(block, axis, [(k, (k + s) % n) for k in range(n)])


def order_body(n, axis, at_ref, *refs):
    pieces, out = refs[:n], refs[n]
    for t in range(n):
        out[lax.rem(at_ref[axis] + (n - t), n)] = pieces[t][...]


def copy_body(at_ref, in_ref, out_ref):
    out_ref[...] = in_ref[...]


def split_body(n, tokens_ref, out_ref, done):
    width = tokens_ref.shape[1] // n
    copies = [
        pltpu.make_async_copy(tokens_ref.at[:, pl.ds(k * width, width)], out_ref.at[k], done.at[k]) for k in range(n)
    ]
    for copy in copies:
        copy.start()
    for copy in copies:
        copy.wait()


def on_vmem(body, outs, flops, moved, at, *operands, after=()):
    skip = len(after)

    def called(at_ref, *refs):
        body(at_ref, *refs[skip:])

    return pl.pallas_call(
        called,
        out_shape=outs,
        in_specs=[SMEM] + [ANY] * skip + [VMEM] * len(operands),
        out_specs=jax.tree.map(lambda _: VMEM, outs),
        compiler_params=pltpu.CompilerParams(vmem_limit_bytes=VMEM_LIMIT),
        cost_estimate=pl.CostEstimate(flops=flops, bytes_accessed=moved, transcendentals=0),
    )(at, *after, *operands)


def outer_body(replicas, at_ref, mine_ref, sent_ref, came_ref, params_ref, moment_ref, params_out, moment_out, pair_out):
    half, which = at_ref[2], at_ref[3]

    def step(g, m, summed):
        outer_grad = g - summed / replicas
        moment = moment_keep * m + outer_grad
        return g - outer_rate * (outer_grad + moment_keep * moment), moment

    here, moment = step(sent_ref[1], sent_ref[2], mine_ref[...] + came_ref[0])
    there, _ = step(came_ref[1], came_ref[2], came_ref[3] + sent_ref[0])
    params_out[...] = params_ref[...]
    moment_out[...] = moment_ref[...]
    params_out[which] = here
    moment_out[which] = moment
    pair_out[half] = here
    pair_out[1 - half] = there


def base_body(at_ref, rows_ref, spread_ref, out_ref):
    nz, nc, nh, piece, _ = spread_ref.shape
    for z in range(nz):
        for h in range(nh):
            for c in range(nc):
                first = ((z * nh + h) * nc + c) * piece
                own = rows_ref[pl.ds(first, piece), :]
                out_ref[pl.ds(first, piece), :] = merge_share * own + (1.0 - merge_share) * spread_ref[z, c, h]


def f32(*shape):
    return jax.ShapeDtypeStruct(shape, jnp.float32)


def on_device(inputs, targets, local_weight, outer_params, outer_moment, fragment):
    which = jnp.remainder(fragment[0], jnp.int32(outer_params.shape[0]))
    own_rows, tokens, wanted = local_weight[0], inputs[0], targets[0]
    rows, width = own_rows.shape
    count = tokens.shape[0]
    n = lax.axis_size("x")
    nz, nh, nc = (lax.axis_size(a) for a in REPLICA)
    piece = rows // (nz * nh * nc)
    half = lax.axis_index("yh")
    at = jnp.stack([lax.axis_index("x"), lax.axis_index("yl"), half, which]).astype(jnp.int32)
    features = tokens.shape[1] // n
    chunks = [slice(a, b) for a, b in zip(CUTS, CUTS[1:])]
    parts = [c.stop - c.start for c in chunks]
    last = len(chunks) - 1

    def hold(x, after):
        return on_vmem(copy_body, jax.ShapeDtypeStruct(x.shape, x.dtype), 0, x.size * 4, at, x, after=after)

    def in_order(pieces, axis, after=()):
        shape = (n,) + pieces[0].shape
        out = jax.ShapeDtypeStruct(shape, pieces[0].dtype)
        body = functools.partial(order_body, n, axis)
        return on_vmem(body, out, 0, 1 << 21, at, *pieces, after=after).reshape(n * shape[1], shape[2])

    blocks = pl.pallas_call(
        functools.partial(split_body, n),
        out_shape=jax.ShapeDtypeStruct((n, count, features), tokens.dtype),
        in_specs=[ANY],
        out_specs=VMEM,
        scratch_shapes=[pltpu.SemaphoreType.DMA((n,))],
        compiler_params=pltpu.CompilerParams(vmem_limit_bytes=VMEM_LIMIT),
    )(tokens)
    block = rowwise(exchange(blocks, "x").reshape(n * count, features))
    rows_now = hold(own_rows, [blocks])
    pieces = [[rows_now[:, c]] for c in chunks]
    for held in pieces:
        held.extend(shift(held[0], "yl", s) for s in range(1, n))
    weights = [in_order(pieces[0], 1, after=[pieces[1][1]])]

    core = lax.axis_index("core")
    by_owner = rows_now.reshape(nz, nh, nc, piece, width)
    sent = lax.dynamic_index_in_dim(by_owner, 1 - core, 2, keepdims=False)
    here = lax.dynamic_index_in_dim(by_owner, core, 2, keepdims=False).astype(jnp.float32)
    here = here + lax.ppermute(sent, "core", [(0, 1), (1, 0)]).astype(jnp.float32)
    part = lax.psum_scatter(here, "z", scatter_dimension=0, tiled=True)[0]

    part = on_vmem(copy_body, f32(*part.shape), EARLY, 1 << 18, at, part)

    def project(k):
        shares = jnp.dot(block, weights[k], preferred_element_type=jnp.float32)
        return rowwise((shares * SHARE_UP).astype(WIRE)).reshape(n, count, -1)

    def residual_of(got, aims):
        got = [got[k].astype(jnp.float32) for k in range(n)]
        projected = ((got[0] + got[1]) + (got[2] + got[3])) * (1.0 / SHARE_UP)
        return (projected - aims.astype(jnp.float32)).astype(jnp.bfloat16)

    def gradient(res):
        shares = lax.dot_general(
            block, rowwise(res.reshape(n * count, -1)), (((0,), (0,)), ((), ())), preferred_element_type=jnp.float32
        )
        return rowwise((shares * GRAD_DOWN).astype(WIRE)).reshape(n, rows, -1)

    whole = []
    for k, c in enumerate(chunks):
        aims = wanted[:, c] if k == 0 else hold(wanted[:, c], [residual])
        shares = project(k)
        if k < last:
            weights.append(in_order(pieces[k + 1], 1, after=[shares[0, :8, :128].astype(jnp.float32)]))
        residual = residual_of(exchange(shares, "x"), aims)
        if k == 0:
            residual = hold(residual, [part])
        whole.append(in_order([residual] + [shift(residual, "x", s) for s in range(1, n)], 0))

    g_piece = lax.dynamic_index_in_dim(outer_params, which, 0, keepdims=False)
    m_piece = lax.dynamic_index_in_dim(outer_moment, which, 0, keepdims=False)
    mine = lax.dynamic_index_in_dim(part, half, 0, keepdims=False)
    other = lax.dynamic_index_in_dim(part, 1 - half, 0, keepdims=False)
    sent = jnp.stack([other, g_piece, m_piece, mine])
    came = lax.ppermute(sent, "yh", [(0, 1), (1, 0)])
    new_params, new_moment, pair = on_vmem(
        functools.partial(outer_body, nz * nh * nc),
        [f32(*outer_params.shape), f32(*outer_moment.shape), f32(nh, piece, width)],
        0, 1 << 20, at, mine, sent, came, outer_params, outer_moment,
    )
    spread = lax.all_gather(pair, ("z", "core"), axis=0, tiled=False).reshape(nz, nc, nh, piece, width)

    gradients = []
    whole[0] = hold(whole[0], [pair])
    for k in range(last + 1):
        if k == last:
            base = on_vmem(base_body, f32(rows, width), 0, 1 << 22, at, own_rows.astype(jnp.float32), spread)
        got = exchange(gradient(whole[k]), "yl")
        got = [got[j].astype(jnp.float32) for j in range(n)]
        gradients.append((got[0] + got[1]) + (got[2] + got[3]))
    step = merge_share * inner_rate / (count * n * n * GRAD_DOWN)
    merged = base - step * jnp.concatenate(gradients, axis=1)
    return (merged[None], new_params, new_moment)


def solution(mesh):
    names = tuple(n for n, _ in PARTS)
    fine = Mesh(mesh.devices.reshape([k for _, k in PARTS]), names)
    local = P(REPLICA, FSDP, None)
    outer = P(None, FSDP + REPLICA, None)
    return jax.shard_map(
        on_device,
        mesh=fine,
        in_specs=(local, local, local, outer, outer, P()),
        out_specs=(local, outer, outer),
        check_vma=False,
    )
```

```python
import functools

import jax
import jax.numpy as jnp
from jax import lax
from jax.experimental import pallas as pl
from jax.experimental.layout import Layout, with_layout_constraint
from jax.experimental.pallas import tpu as pltpu
from jax.sharding import Mesh, PartitionSpec as P

inner_rate = 1.0
outer_rate = 0.7
moment_keep = 0.9
merge_share = 0.5

PARTS = (("z", 8), ("yh", 2), ("core", 2), ("x", 4), ("yl", 4))
REPLICA = ("z", "yh", "core")
FSDP = ("x", "yl")
CUTS = (0, 512, 1024)
WIRE = jnp.float16
SHARE_UP = 32.0
GRAD_DOWN = 2.0**-8
EARLY = 30_000_000_000
VMEM_LIMIT = 12 << 20
VMEM = pl.BlockSpec(memory_space=pltpu.VMEM)
ANY = pl.BlockSpec(memory_space=pl.ANY)
SMEM = pl.BlockSpec(memory_space=pltpu.SMEM)


def exchange(blocks, axis):
    return lax.all_to_all(blocks, axis, 0, 0, tiled=True)


def rowwise(x):
    return with_layout_constraint(x, Layout(tuple(range(x.ndim))))


def shift(block, axis, s):
    n = lax.axis_size(axis)
    return lax.ppermute(block, axis, [(k, (k + s) % n) for k in range(n)])


def order_body(n, axis, at_ref, *refs):
    pieces, out = refs[:n], refs[n]
    for t in range(n):
        out[lax.rem(at_ref[axis] + (n - t), n)] = pieces[t][...]


def copy_body(at_ref, in_ref, out_ref):
    out_ref[...] = in_ref[...]


def split_body(n, tokens_ref, out_ref, done):
    width = tokens_ref.shape[1] // n
    copies = [
        pltpu.make_async_copy(tokens_ref.at[:, pl.ds(k * width, width)], out_ref.at[k], done.at[k]) for k in range(n)
    ]
    for copy in copies:
        copy.start()
    for copy in copies:
        copy.wait()


def on_vmem(body, outs, flops, moved, at, *operands, after=()):
    skip = len(after)

    def called(at_ref, *refs):
        body(at_ref, *refs[skip:])

    return pl.pallas_call(
        called,
        out_shape=outs,
        in_specs=[SMEM] + [ANY] * skip + [VMEM] * len(operands),
        out_specs=jax.tree.map(lambda _: VMEM, outs),
        compiler_params=pltpu.CompilerParams(vmem_limit_bytes=VMEM_LIMIT),
        cost_estimate=pl.CostEstimate(flops=flops, bytes_accessed=moved, transcendentals=0),
    )(at, *after, *operands)


def outer_body(replicas, at_ref, mine_ref, sent_ref, came_ref, params_ref, moment_ref, params_out, moment_out, pair_out):
    half, which = at_ref[2], at_ref[3]

    def step(g, m, summed):
        outer_grad = g - summed / replicas
        moment = moment_keep * m + outer_grad
        return g - outer_rate * (outer_grad + moment_keep * moment), moment

    here, moment = step(sent_ref[1], sent_ref[2], mine_ref[...] + came_ref[0])
    there, _ = step(came_ref[1], came_ref[2], came_ref[3] + sent_ref[0])
    params_out[...] = params_ref[...]
    moment_out[...] = moment_ref[...]
    params_out[which] = here
    moment_out[which] = moment
    pair_out[half] = here
    pair_out[1 - half] = there


def base_body(at_ref, rows_ref, spread_ref, out_ref):
    nz, nc, nh, piece, _ = spread_ref.shape
    for z in range(nz):
        for h in range(nh):
            for c in range(nc):
                first = ((z * nh + h) * nc + c) * piece
                own = rows_ref[pl.ds(first, piece), :]
                out_ref[pl.ds(first, piece), :] = merge_share * own + (1.0 - merge_share) * spread_ref[z, c, h]


def f32(*shape):
    return jax.ShapeDtypeStruct(shape, jnp.float32)


def on_device(inputs, targets, local_weight, outer_params, outer_moment, fragment):
    which = jnp.remainder(fragment[0], jnp.int32(outer_params.shape[0]))
    own_rows, tokens, wanted = local_weight[0], inputs[0], targets[0]
    rows, width = own_rows.shape
    count = tokens.shape[0]
    n = lax.axis_size("x")
    nz, nh, nc = (lax.axis_size(a) for a in REPLICA)
    piece = rows // (nz * nh * nc)
    half = lax.axis_index("yh")
    at = jnp.stack([lax.axis_index("x"), lax.axis_index("yl"), half, which]).astype(jnp.int32)
    features = tokens.shape[1] // n
    chunks = [slice(a, b) for a, b in zip(CUTS, CUTS[1:])]
    parts = [c.stop - c.start for c in chunks]
    last = len(chunks) - 1

    def hold(x, after):
        return on_vmem(copy_body, jax.ShapeDtypeStruct(x.shape, x.dtype), 0, x.size * 4, at, x, after=after)

    def in_order(pieces, axis, after=()):
        shape = (n,) + pieces[0].shape
        out = jax.ShapeDtypeStruct(shape, pieces[0].dtype)
        body = functools.partial(order_body, n, axis)
        return on_vmem(body, out, 0, 1 << 21, at, *pieces, after=after).reshape(n * shape[1], shape[2])

    blocks = pl.pallas_call(
        functools.partial(split_body, n),
        out_shape=jax.ShapeDtypeStruct((n, count, features), tokens.dtype),
        in_specs=[ANY],
        out_specs=VMEM,
        scratch_shapes=[pltpu.SemaphoreType.DMA((n,))],
        compiler_params=pltpu.CompilerParams(vmem_limit_bytes=VMEM_LIMIT),
    )(tokens)
    block = rowwise(exchange(blocks, "x").reshape(n * count, features))
    rows_now = hold(own_rows, [blocks])
    pieces = [[rows_now[:, c]] for c in chunks]
    for held in pieces:
        held.extend(shift(held[0], "yl", s) for s in range(1, n))
    weights = [in_order(pieces[0], 1, after=[pieces[1][1]])]

    core = lax.axis_index("core")
    by_owner = rows_now.reshape(nz, nh, nc, piece, width)
    sent = lax.dynamic_index_in_dim(by_owner, 1 - core, 2, keepdims=False)
    here = lax.dynamic_index_in_dim(by_owner, core, 2, keepdims=False).astype(jnp.float32)
    here = here + lax.ppermute(sent, "core", [(0, 1), (1, 0)]).astype(jnp.float32)
    part = lax.psum_scatter(here, "z", scatter_dimension=0, tiled=True)[0]

    part = on_vmem(copy_body, f32(*part.shape), EARLY, 1 << 18, at, part)

    def project(k):
        shares = jnp.dot(block, weights[k], preferred_element_type=jnp.float32)
        return rowwise((shares * SHARE_UP).astype(WIRE)).reshape(n, count, -1)

    def residual_of(got, aims):
        got = [got[k].astype(jnp.float32) for k in range(n)]
        projected = ((got[0] + got[1]) + (got[2] + got[3])) * (1.0 / SHARE_UP)
        return (projected - aims.astype(jnp.float32)).astype(jnp.bfloat16)

    def gradient(res):
        shares = lax.dot_general(
            block, rowwise(res.reshape(n * count, -1)), (((0,), (0,)), ((), ())), preferred_element_type=jnp.float32
        )
        return rowwise((shares * GRAD_DOWN).astype(WIRE)).reshape(n, rows, -1)

    whole = []
    for k, c in enumerate(chunks):
        aims = wanted[:, c] if k == 0 else hold(wanted[:, c], [residual])
        shares = project(k)
        if k < last:
            weights.append(in_order(pieces[k + 1], 1, after=[shares[0, :8, :128].astype(jnp.float32)]))
        residual = residual_of(exchange(shares, "x"), aims)
        if k == 0:
            residual = hold(residual, [part])
        whole.append(in_order([residual] + [shift(residual, "x", s) for s in range(1, n)], 0))

    g_piece = lax.dynamic_index_in_dim(outer_params, which, 0, keepdims=False)
    m_piece = lax.dynamic_index_in_dim(outer_moment, which, 0, keepdims=False)
    mine = lax.dynamic_index_in_dim(part, half, 0, keepdims=False)
    other = lax.dynamic_index_in_dim(part, 1 - half, 0, keepdims=False)
    sent = jnp.stack([other, g_piece, m_piece, mine])
    came = lax.ppermute(sent, "yh", [(0, 1), (1, 0)])
    new_params, new_moment, pair = on_vmem(
        functools.partial(outer_body, nz * nh * nc),
        [f32(*outer_params.shape), f32(*outer_moment.shape), f32(nh, piece, width)],
        0, 1 << 20, at, mine, sent, came, outer_params, outer_moment,
    )
    spread = lax.all_gather(pair, ("z", "core"), axis=0, tiled=False).reshape(nz, nc, nh, piece, width)

    gradients = []
    whole[0] = hold(whole[0], [came])
    for k in range(last + 1):
        if k == last:
            base = on_vmem(base_body, f32(rows, width), 0, 1 << 22, at, own_rows.astype(jnp.float32), spread)
        got = exchange(gradient(whole[k]), "yl")
        got = [got[j].astype(jnp.float32) for j in range(n)]
        gradients.append((got[0] + got[1]) + (got[2] + got[3]))
    step = merge_share * inner_rate / (count * n * n * GRAD_DOWN)
    merged = base - step * jnp.concatenate(gradients, axis=1)
    return (merged[None], new_params, new_moment)


def solution(mesh):
    names = tuple(n for n, _ in PARTS)
    fine = Mesh(mesh.devices.reshape([k for _, k in PARTS]), names)
    local = P(REPLICA, FSDP, None)
    outer = P(None, FSDP + REPLICA, None)
    return jax.shard_map(
        on_device,
        mesh=fine,
        in_specs=(local, local, local, outer, outer, P()),
        out_specs=(local, outer, outer),
        check_vma=False,
    )
```

```python
import functools

import jax
import jax.numpy as jnp
from jax import lax
from jax.experimental import pallas as pl
from jax.experimental.layout import Layout, with_layout_constraint
from jax.experimental.pallas import tpu as pltpu
from jax.sharding import Mesh, PartitionSpec as P

inner_rate = 1.0
outer_rate = 0.7
moment_keep = 0.9
merge_share = 0.5

PARTS = (("z", 8), ("yh", 2), ("core", 2), ("x", 4), ("yl", 4))
REPLICA = ("z", "yh", "core")
FSDP = ("x", "yl")
CUTS = (0, 512, 1024)
WIRE = jnp.float16
SHARE_UP = 32.0
GRAD_DOWN = 2.0**-8
EARLY = 30_000_000_000
VMEM_LIMIT = 12 << 20
VMEM = pl.BlockSpec(memory_space=pltpu.VMEM)
ANY = pl.BlockSpec(memory_space=pl.ANY)
SMEM = pl.BlockSpec(memory_space=pltpu.SMEM)


def exchange(blocks, axis):
    return lax.all_to_all(blocks, axis, 0, 0, tiled=True)


def rowwise(x):
    return with_layout_constraint(x, Layout(tuple(range(x.ndim))))


def shift(block, axis, s):
    n = lax.axis_size(axis)
    return lax.ppermute(block, axis, [(k, (k + s) % n) for k in range(n)])


def order_body(n, axis, at_ref, *refs):
    pieces, out, done = refs[:n], refs[n], refs[n + 1]
    copies = [
        pltpu.make_async_copy(pieces[t], out.at[lax.rem(at_ref[axis] + (n - t), n)], done.at[t]) for t in range(n)
    ]
    for copy in copies:
        copy.start()
    for copy in copies:
        copy.wait()


def copy_body(at_ref, in_ref, out_ref):
    out_ref[...] = in_ref[...]


def split_body(n, tokens_ref, out_ref, done):
    width = tokens_ref.shape[1] // n
    copies = [
        pltpu.make_async_copy(tokens_ref.at[:, pl.ds(k * width, width)], out_ref.at[k], done.at[k]) for k in range(n)
    ]
    for copy in copies:
        copy.start()
    for copy in copies:
        copy.wait()


def on_vmem(body, outs, flops, moved, at, *operands, after=()):
    skip = len(after)

    def called(at_ref, *refs):
        body(at_ref, *refs[skip:])

    return pl.pallas_call(
        called,
        out_shape=outs,
        in_specs=[SMEM] + [ANY] * skip + [VMEM] * len(operands),
        out_specs=jax.tree.map(lambda _: VMEM, outs),
        compiler_params=pltpu.CompilerParams(vmem_limit_bytes=VMEM_LIMIT),
        cost_estimate=pl.CostEstimate(flops=flops, bytes_accessed=moved, transcendentals=0),
    )(at, *after, *operands)


def outer_body(replicas, at_ref, mine_ref, sent_ref, came_ref, params_ref, moment_ref, params_out, moment_out, pair_out):
    half, which = at_ref[2], at_ref[3]

    def step(g, m, summed):
        outer_grad = g - summed / replicas
        moment = moment_keep * m + outer_grad
        return g - outer_rate * (outer_grad + moment_keep * moment), moment

    here, moment = step(sent_ref[1], sent_ref[2], mine_ref[...] + came_ref[0])
    there, _ = step(came_ref[1], came_ref[2], came_ref[3] + sent_ref[0])
    params_out[...] = params_ref[...]
    moment_out[...] = moment_ref[...]
    params_out[which] = here
    moment_out[which] = moment
    pair_out[half] = here
    pair_out[1 - half] = there


def base_body(at_ref, rows_ref, spread_ref, out_ref):
    nz, nc, nh, piece, _ = spread_ref.shape
    for z in range(nz):
        for h in range(nh):
            for c in range(nc):
                first = ((z * nh + h) * nc + c) * piece
                own = rows_ref[pl.ds(first, piece), :]
                out_ref[pl.ds(first, piece), :] = merge_share * own + (1.0 - merge_share) * spread_ref[z, c, h]


def f32(*shape):
    return jax.ShapeDtypeStruct(shape, jnp.float32)


def on_device(inputs, targets, local_weight, outer_params, outer_moment, fragment):
    which = jnp.remainder(fragment[0], jnp.int32(outer_params.shape[0]))
    own_rows, tokens, wanted = local_weight[0], inputs[0], targets[0]
    rows, width = own_rows.shape
    count = tokens.shape[0]
    n = lax.axis_size("x")
    nz, nh, nc = (lax.axis_size(a) for a in REPLICA)
    piece = rows // (nz * nh * nc)
    half = lax.axis_index("yh")
    at = jnp.stack([lax.axis_index("x"), lax.axis_index("yl"), half, which]).astype(jnp.int32)
    features = tokens.shape[1] // n
    chunks = [slice(a, b) for a, b in zip(CUTS, CUTS[1:])]
    parts = [c.stop - c.start for c in chunks]
    last = len(chunks) - 1

    def hold(x, after):
        return on_vmem(copy_body, jax.ShapeDtypeStruct(x.shape, x.dtype), 0, x.size * 4, at, x, after=after)

    def in_order(pieces, axis, after=()):
        shape = (n,) + pieces[0].shape
        skip = len(after)

        def called(at_ref, *refs):
            order_body(n, axis, at_ref, *refs[skip:])

        return pl.pallas_call(
            called,
            out_shape=jax.ShapeDtypeStruct(shape, pieces[0].dtype),
            in_specs=[SMEM] + [ANY] * (skip + n),
            out_specs=VMEM,
            scratch_shapes=[pltpu.SemaphoreType.DMA((n,))],
            compiler_params=pltpu.CompilerParams(vmem_limit_bytes=VMEM_LIMIT),
        )(at, *after, *pieces).reshape(n * shape[1], shape[2])

    blocks = pl.pallas_call(
        functools.partial(split_body, n),
        out_shape=jax.ShapeDtypeStruct((n, count, features), tokens.dtype),
        in_specs=[ANY],
        out_specs=VMEM,
        scratch_shapes=[pltpu.SemaphoreType.DMA((n,))],
        compiler_params=pltpu.CompilerParams(vmem_limit_bytes=VMEM_LIMIT),
    )(tokens)
    block = rowwise(exchange(blocks, "x").reshape(n * count, features))
    rows_now = hold(own_rows, [blocks])
    pieces = [[rows_now[:, c]] for c in chunks]
    for held in pieces:
        held.extend(shift(held[0], "yl", s) for s in range(1, n))
    weights = [in_order(pieces[0], 1, after=[pieces[1][1]])]

    core = lax.axis_index("core")
    by_owner = rows_now.reshape(nz, nh, nc, piece, width)
    sent = lax.dynamic_index_in_dim(by_owner, 1 - core, 2, keepdims=False)
    here = lax.dynamic_index_in_dim(by_owner, core, 2, keepdims=False).astype(jnp.float32)
    here = here + lax.ppermute(sent, "core", [(0, 1), (1, 0)]).astype(jnp.float32)
    part = lax.psum_scatter(here, "z", scatter_dimension=0, tiled=True)[0]

    part = on_vmem(copy_body, f32(*part.shape), EARLY, 1 << 18, at, part)

    def project(k):
        shares = jnp.dot(block, weights[k], preferred_element_type=jnp.float32)
        return rowwise((shares * SHARE_UP).astype(WIRE)).reshape(n, count, -1)

    def residual_of(got, aims):
        got = [got[k].astype(jnp.float32) for k in range(n)]
        projected = ((got[0] + got[1]) + (got[2] + got[3])) * (1.0 / SHARE_UP)
        return (projected - aims.astype(jnp.float32)).astype(jnp.bfloat16)

    def gradient(res):
        shares = lax.dot_general(
            block, rowwise(res.reshape(n * count, -1)), (((0,), (0,)), ((), ())), preferred_element_type=jnp.float32
        )
        return rowwise((shares * GRAD_DOWN).astype(WIRE)).reshape(n, rows, -1)

    whole = []
    for k, c in enumerate(chunks):
        aims = wanted[:, c] if k == 0 else hold(wanted[:, c], [residual])
        shares = project(k)
        if k < last:
            weights.append(in_order(pieces[k + 1], 1, after=[shares[0, :8, :128].astype(jnp.float32), part]))
        residual = residual_of(exchange(shares, "x"), aims)
        whole.append(in_order([residual] + [shift(residual, "x", s) for s in range(1, n)], 0))

    g_piece = lax.dynamic_index_in_dim(outer_params, which, 0, keepdims=False)
    m_piece = lax.dynamic_index_in_dim(outer_moment, which, 0, keepdims=False)
    mine = lax.dynamic_index_in_dim(part, half, 0, keepdims=False)
    other = lax.dynamic_index_in_dim(part, 1 - half, 0, keepdims=False)
    sent = jnp.stack([other, g_piece, m_piece, mine])
    came = lax.ppermute(sent, "yh", [(0, 1), (1, 0)])
    new_params, new_moment, pair = on_vmem(
        functools.partial(outer_body, nz * nh * nc),
        [f32(*outer_params.shape), f32(*outer_moment.shape), f32(nh, piece, width)],
        0, 1 << 20, at, mine, sent, came, outer_params, outer_moment,
    )
    spread = lax.all_gather(pair, ("z", "core"), axis=0, tiled=False).reshape(nz, nc, nh, piece, width)

    gradients = []
    whole[0] = hold(whole[0], [came])
    for k in range(last + 1):
        if k == last:
            base = on_vmem(base_body, f32(rows, width), 0, 1 << 22, at, own_rows.astype(jnp.float32), spread)
        got = exchange(gradient(whole[k]), "yl")
        got = [got[j].astype(jnp.float32) for j in range(n)]
        gradients.append((got[0] + got[1]) + (got[2] + got[3]))
    step = merge_share * inner_rate / (count * n * n * GRAD_DOWN)
    merged = base - step * jnp.concatenate(gradients, axis=1)
    return (merged[None], new_params, new_moment)


def solution(mesh):
    names = tuple(n for n, _ in PARTS)
    fine = Mesh(mesh.devices.reshape([k for _, k in PARTS]), names)
    local = P(REPLICA, FSDP, None)
    outer = P(None, FSDP + REPLICA, None)
    return jax.shard_map(
        on_device,
        mesh=fine,
        in_specs=(local, local, local, outer, outer, P()),
        out_specs=(local, outer, outer),
        check_vma=False,
    )
```
